32 devices in a mesh: tm: 16 (over z, x, core), mp: 2 (over y).
Axes of the slice: x: 2, y: 2, z: 4, core: 2. Of those that a mesh axis runs over, the one named last changes fastest.
Arguments:
- tokens: bfloat16 [4096, 1024], P('tm'), may hold values from -9 to 9
- norm1_gain: float32 [1024], replicated, may hold values from 0.5 to 1.5
- query_weight: bfloat16 [1024, 1024], P(None, 'mp'), may hold values from -1 to 1
- key_weight: bfloat16 [1024, 1024], P(None, 'mp'), may hold values from -1 to 1
- value_weight: bfloat16 [1024, 1024], P(None, 'mp'), may hold values from -0.1875 to 0.1875
- output_weight: bfloat16 [1024, 1024], P('mp'), may hold values from -5 to 5
- pattern: int32 [32, 8], replicated, may hold values from -1 to 31, as said below
- adjacency: int32 [128, 128], replicated, may hold values 0 or 1
- decay_rate: float32 [1024], P('mp'), may hold values from 0.015625 to 0.1
- norm2_gain: float32 [1024], replicated, may hold values from 0.5 to 1.5
- up_weight: bfloat16 [1024, 4096], P(None, 'mp'), may hold values from -0.1875 to 0.1875
- down_weight: bfloat16 [4096, 1024], P('mp'), may hold values from -0.09375 to 0.09375
Outputs:
- layer_out: bfloat16 [4096, 1024], P('tm', 'mp')
The draws below stay inside these ranges and needn't reach their ends.
Inputs may be any that keep to these rules, and one draw needn't show every extreme that they name: pattern[b, 0] = b and pattern[b, 1] = b - 1. For the rows of the blocks g * 2 to g * 2 + 1, entry 2 + k (k from 0 to 5) is the same in all these rows: -1 where g < 2^k, else one of the blocks (g - 2^k) * 2 to (g - 2^k) * 2 + 1, never the block g * 2 - 1.
All inputs are finite; a program needn't handle non-finite values.
Results may differ from the reference program's by a relative error of at most 0.01.
Values may be sent and summed in bfloat16 or wider, within the bound.
A program may use at most 64 MiB of HBM per device.

```python
import math
import jax
import jax.numpy as jnp
from jax import lax

D = 1024
HEADS = 8
HD = 128
FF = 4096
SITES = 128
STEP_DEV = 2
GLOBAL = 6
TIME = 32
TOKENS = 4096


def drawn_projection(key, salt):
    noise = jax.random.truncated_normal(jax.random.fold_in(key, salt), -6.0, 6.0, (D, HEADS * HD), jnp.float32)
    return noise * (1.0 / math.sqrt(D))


def draw_tokens(key, part):
    noise = jax.random.truncated_normal(jax.random.fold_in(key, 1), -6.0, 6.0, (TOKENS, D), jnp.float32)
    return noise.astype(jnp.bfloat16)


def draw_query_weight(key, part):
    return drawn_projection(key, 11).astype(jnp.bfloat16)


def draw_key_weight(key, part):
    return drawn_projection(key, 13).astype(jnp.bfloat16)


def draw_pattern(key, part):
    groups = TIME // STEP_DEV
    base = jax.random.fold_in(key, 7)
    group_ids = jnp.arange(groups, dtype=jnp.int32)[:, None]
    powers = jnp.left_shift(jnp.ones((GLOBAL,), jnp.int32), jnp.arange(GLOBAL, dtype=jnp.int32))[None, :]
    sources = group_ids - powers
    limits = jnp.broadcast_to(jnp.where(jnp.arange(GLOBAL, dtype=jnp.int32)[None, :] == 0, STEP_DEV - 1, STEP_DEV), (groups, GLOBAL)).astype(jnp.int32)
    offsets = jax.random.randint(base, (groups, GLOBAL), 0, limits).astype(jnp.int32)
    blocks = jnp.where(sources >= 0, sources * STEP_DEV + offsets, -1).astype(jnp.int32)
    remote = jnp.broadcast_to(blocks[:, None, :], (groups, STEP_DEV, GLOBAL)).reshape(TIME, GLOBAL)
    steps_all = jnp.arange(TIME, dtype=jnp.int32)[:, None]
    return jnp.concatenate([steps_all, steps_all - 1, remote], axis=1).astype(jnp.int32)


def set_ends(values, key, low, high):
    longest = values.shape.index(max(values.shape))
    spots = []
    for shift in (0, 1):
        where = [jax.random.randint(jax.random.fold_in(key, axis), (), 0, length) for axis, length in enumerate(values.shape)]
        where[longest] = (where[longest] + shift) % values.shape[longest]
        spots.append(tuple(where))
    return values.at[spots[0]].set(low).at[spots[1]].set(high)


def steps_of(key, extent, shards, smallest, high):
    level, own = 1.0, jax.random.fold_in(key, 6)
    for dim, parts in shards:
        steps = jnp.exp(jax.random.uniform(jax.random.fold_in(own, dim), (parts,), jnp.float32, smallest / len(shards), high / len(shards)))
        level = level * jnp.repeat(steps, extent[dim] // parts).reshape([-1 if axis == dim else 1 for axis in range(len(extent))])
    return level


def normal_values(rng, extent, scale, most, cuts=(), kind=jnp.bfloat16):
    loudness = steps_of(rng, extent, cuts, -0.22, 0.18) if cuts else 1.0
    values = jax.random.normal(rng, extent, jnp.float32) * scale * loudness
    return jnp.minimum(jnp.maximum(values, -most), most).astype(kind)


def setup_inputs(seed: int = 0) -> dict:
    splits = jax.random.split(jax.random.key(seed), 13)
    return {
        "tokens": draw_tokens(jax.random.fold_in(splits[12], 71), 0),
        "norm1_gain": jnp.clip(1.0 + 0.1 * jax.random.normal(splits[1], (D,), jnp.float32), 0.5, 1.5),
        "query_weight": draw_query_weight(jax.random.fold_in(splits[12], 71), 0),
        "key_weight": draw_key_weight(jax.random.fold_in(splits[12], 71), 0),
        "value_weight": normal_values(splits[4], (D, HEADS * HD), D ** -0.5, 0.1875, ((1, 2),)),
        "output_weight": normal_values(splits[5], (HEADS * HD, D), 0.35, 5.0, ((0, 2),)),
        "pattern": draw_pattern(jax.random.fold_in(splits[12], 71), 0),
        "adjacency": set_ends((jax.random.randint(splits[7], (SITES, SITES), 0, SITES) < 8).astype(jnp.int32), jax.random.fold_in(splits[7], 1), 0, 1),
        "decay_rate": jnp.clip(jnp.exp(math.log(0.1) - 1.856298 * jax.random.uniform(splits[8], (D,), jnp.float32) ** steps_of(splits[8], (D,), ((0, 2),), -0.2, 0.2)), 0.015625, 0.1),
        "norm2_gain": jnp.clip(1.0 + 0.1 * jax.random.normal(splits[9], (D,), jnp.float32), 0.5, 1.5),
        "up_weight": normal_values(splits[10], (D, FF), D ** -0.5, 0.1875, ((1, 2),)),
        "down_weight": normal_values(splits[11], (FF, D), FF ** -0.5, 0.09375, ((0, 2),)),
    }


highest = lax.Precision.HIGHEST

def rms_norm(rows, gain):
    widened = rows.astype(jnp.float32)
    square = lax.optimization_barrier(jnp.mean(widened * widened, axis=-1, keepdims=True))
    return (widened * lax.rsqrt(square + 1e-05) * gain.astype(jnp.float32)).astype(jnp.bfloat16)

def block_partial(queries, key_rows, value_rows, heads):
    head_size = queries.shape[-1] // heads
    query_split = queries.astype(jnp.float32).reshape(queries.shape[:-1] + (heads, head_size))
    key_split = key_rows.astype(jnp.float32).reshape(key_rows.shape[:-1] + (heads, head_size))
    value_split = value_rows.astype(jnp.float32).reshape(value_rows.shape[:-1] + (heads, head_size))
    scores = jnp.einsum('...qhd,...khd->...hqk', query_split, key_split, precision=highest) * (1.0 / math.sqrt(head_size))
    tops = lax.optimization_barrier(jnp.max(scores, axis=-1))
    probs = jnp.exp(scores - tops[..., None])
    totals = lax.optimization_barrier(jnp.sum(probs, axis=-1))
    weights = probs.astype(jnp.bfloat16)
    outputs = jnp.einsum('...hqk,...khd->...qhd', weights.astype(jnp.float32), value_split, precision=highest)
    return (tops, totals, outputs.reshape(outputs.shape[:-2] + (heads * head_size,)))

def merge_partials(tops, totals, outputs, valid, heads):
    flags = valid[..., None, None]
    masked = jnp.where(flags, tops, -jnp.inf)
    largest = lax.optimization_barrier(jnp.max(masked, axis=-3))
    factor = jnp.where(flags, jnp.exp(jnp.where(flags, tops, 0.0) - largest[..., None, :, :]), 0.0)
    denom = lax.optimization_barrier(jnp.sum(factor * totals, axis=-3))
    split = outputs.reshape(outputs.shape[:-1] + (heads, -1))
    numer = lax.optimization_barrier(jnp.sum(jnp.swapaxes(factor, -1, -2)[..., None] * split, axis=-4))
    result = numer / jnp.swapaxes(denom, -1, -2)[..., None]
    return result.reshape(result.shape[:-2] + (-1,)).astype(jnp.bfloat16)

def reference(tokens, norm1_gain, query_weight, key_weight, value_weight, output_weight, pattern, adjacency, decay_rate, norm2_gain, up_weight, down_weight):
    width = query_weight.shape[1]
    normed = rms_norm(tokens, norm1_gain)
    queries = jnp.dot(normed, query_weight, preferred_element_type=jnp.float32).astype(jnp.bfloat16).reshape(TIME, SITES, width)
    key_blocks = jnp.dot(normed, key_weight, preferred_element_type=jnp.float32).astype(jnp.bfloat16).reshape(TIME, SITES, width)
    value_blocks = jnp.dot(normed, value_weight, preferred_element_type=jnp.float32).astype(jnp.bfloat16).reshape(TIME, SITES, width)

    def one_block(inputs):
        query_block, entries = inputs
        chosen = jnp.maximum(entries, 0).astype(jnp.int32)
        keys_sel = key_blocks[chosen]
        values_sel = value_blocks[chosen]
        tops, totals, outputs = block_partial(jnp.broadcast_to(query_block, keys_sel.shape), keys_sel, values_sel, HEADS)
        return merge_partials(tops, totals, outputs, entries >= 0, HEADS)
    attended = lax.map(one_block, (queries, pattern)).reshape(TOKENS, width)
    first = (tokens.astype(jnp.float32) + jnp.dot(attended, output_weight, preferred_element_type=jnp.float32)).astype(jnp.bfloat16)
    links = jnp.maximum(adjacency, jnp.eye(SITES, dtype=jnp.int32))
    degree = lax.optimization_barrier(jnp.sum(links, axis=1)).astype(jnp.float32)
    grid = first.reshape(TIME, SITES, D)
    mixed = (jnp.einsum('st,btc->bsc', links.astype(jnp.float32), grid.astype(jnp.float32), precision=highest) / degree[None, :, None]).astype(jnp.bfloat16)
    retain = jnp.exp(-decay_rate)
    inject = jnp.sqrt(1.0 - retain * retain)

    def advance(state, frame):
        state = retain * state + inject * frame.astype(jnp.float32)
        return (state, state.astype(jnp.bfloat16))
    final_state, smoothed = lax.scan(advance, jnp.zeros((SITES, D), jnp.float32), mixed)
    second = (first.astype(jnp.float32) + smoothed.reshape(TOKENS, D).astype(jnp.float32)).astype(jnp.bfloat16)
    normed_late = rms_norm(second, norm2_gain)
    hidden = jax.nn.gelu(jnp.dot(normed_late, up_weight, preferred_element_type=jnp.float32), approximate=True).astype(jnp.bfloat16)
    return (second.astype(jnp.float32) + jnp.dot(hidden, down_weight, preferred_element_type=jnp.float32)).astype(jnp.bfloat16)
```

```python
import functools
import math

import jax
import jax.numpy as jnp
import numpy as np
from jax import lax
from jax.experimental import pallas as pl
from jax.experimental.pallas import tpu as pltpu
from jax.sharding import PartitionSpec as P

HD = 128
MESH = pl.DeviceIdType.MESH


def dot(a, b):
    return jnp.dot(a, b, preferred_element_type=jnp.float32)


def kernel(
    groups,
    parts,
    spans,
    rows,
    slot,
    tokens,
    gain1,
    pattern,
    decay,
    gain2,
    spread,
    degree,
    gather,
    wq,
    wk,
    wv,
    wo,
    wu,
    wd,
    out,
    qkv_w,
    out_w,
    up_w,
    down_w,
    normed,
    queries,
    kv,
    sel,
    tops,
    totals,
    acc,
    attended,
    proj_send,
    proj_recv,
    first,
    mix,
    got,
    smooth,
    back,
    second,
    hidden,
    ff_send,
    ff_recv,
    w_sem,
    far_s,
    far_r,
    proj_s,
    proj_r,
    mix_s,
    mix_r,
    back_s,
    back_r,
    sec_s,
    sec_r,
    ff_s,
    ff_r,
):
    g = lax.axis_index("tm")
    m = lax.axis_index("mp")
    sites = kv.shape[1]
    width = kv.shape[2] // 2
    heads = width // HD
    cols = out.shape[1]
    units = hidden.shape[1]

    loads = [
        pltpu.make_async_copy(wk, qkv_w.at[:, pl.ds(0, width)], w_sem.at[0]),
        pltpu.make_async_copy(wv, qkv_w.at[:, pl.ds(width, width)], w_sem.at[1]),
        pltpu.make_async_copy(wq, qkv_w.at[:, pl.ds(2 * width, width)], w_sem.at[2]),
        pltpu.make_async_copy(wo, out_w, w_sem.at[3]),
        pltpu.make_async_copy(wu, up_w, w_sem.at[4]),
        pltpu.make_async_copy(wd, down_w, w_sem.at[5]),
    ]
    for load in loads:
        load.start()

    barrier = pltpu.get_barrier_semaphore()

    def greet(step, carry):
        pl.semaphore_signal(
            barrier, inc=1, device_id=(lax.rem(g + step, groups), m), device_id_type=MESH
        )
        return carry

    lax.fori_loop(1, groups, greet, 0)
    for step in range(1, parts):
        pl.semaphore_signal(
            barrier, inc=1, device_id=(g, lax.rem(m + step, parts)), device_id_type=MESH
        )

    wide = tokens[...].astype(jnp.float32)
    square = jnp.mean(wide * wide, axis=-1, keepdims=True)
    normed[...] = (wide * lax.rsqrt(square + 1e-05) * gain1[...]).astype(jnp.bfloat16)

    for j in range(2):
        loads[j].wait()
        product = dot(normed[...], qkv_w[:, pl.ds(j * width, width)]).astype(jnp.bfloat16)
        kv[0, :, pl.ds(j * width, width)] = product[:sites]
        kv[1, :, pl.ds(j * width, width)] = product[sites:]
    for i, span in enumerate(spans[1:]):
        target = jnp.minimum(g + span, groups - 1)
        pick = lax.rem(jnp.maximum(pattern[2 * target, 3 + i], 0), 2).astype(jnp.float32)
        sel[i] = (
            kv[0].astype(jnp.float32) * (1.0 - pick) + kv[1].astype(jnp.float32) * pick
        ).astype(jnp.bfloat16)

    pl.semaphore_wait(barrier, groups + parts - 2)

    def far_copy(i):
        source = kv.at[pl.ds(0, 2)] if i == 0 else sel.at[pl.ds(i - 1, 1)]
        target = kv.at[pl.ds(2, 2)] if i == 0 else kv.at[pl.ds(3 + i, 1)]
        return pltpu.make_async_remote_copy(
            src_ref=source,
            dst_ref=target,
            send_sem=far_s.at[i],
            recv_sem=far_r.at[i],
            device_id=(jnp.minimum(g + spans[i], groups - 1), m),
            device_id_type=MESH,
        )

    for i in reversed(range(len(spans))):

        @pl.when(g + spans[i] < groups)
        def _(i=i):
            far_copy(i).start()

    loads[2].wait()
    queries[...] = dot(normed[...], qkv_w[:, pl.ds(2 * width, width)]).astype(jnp.bfloat16)

    scale = 1.0 / math.sqrt(HD)

    def attend(start, count, hide, fresh):
        for h in range(heads):
            at = pl.ds(h * HD, HD)
            keys = kv[pl.ds(start, count), :, at].reshape(count * sites, HD)
            values = kv[pl.ds(start, count), :, pl.ds(width + h * HD, HD)].reshape(
                count * sites, HD
            )
            scores = (
                lax.dot_general(
                    queries[:, at],
                    keys,
                    (((1,), (1,)), ((), ())),
                    preferred_element_type=jnp.float32,
                )
                * scale
            )
            if hide is not None:
                step = lax.broadcasted_iota(jnp.int32, scores.shape, 0) // sites
                block = lax.broadcasted_iota(jnp.int32, scores.shape, 1) // sites
                scores = jnp.where((step == hide[0]) & (block == hide[1]), -jnp.inf, scores)
            top = jnp.max(scores, axis=-1, keepdims=True)
            if fresh:
                probs = jnp.exp(scores - top)
                total = jnp.sum(probs, axis=-1, keepdims=True)
                part = dot(probs.astype(jnp.bfloat16), values)
            else:
                old = tops[h][:, :1]
                top = jnp.maximum(top, old)
                factor = jnp.exp(old - top)
                probs = jnp.exp(scores - top)
                total = totals[h][:, :1] * factor + jnp.sum(probs, axis=-1, keepdims=True)
                part = acc[:, at] * factor + dot(probs.astype(jnp.bfloat16), values)
            tops[h] = jnp.broadcast_to(top, tops.shape[1:])
            totals[h] = jnp.broadcast_to(total, totals.shape[1:])
            acc[:, at] = part

    attend(0, 2, (0, 1), True)
    for i, span in enumerate(spans):

        @pl.when(g >= span)
        def _(i=i):
            far_copy(i).wait_recv()
            if i == 0:
                attend(2, 2, (1, 1), False)
            else:
                attend(3 + i, 1, None, False)

    for h in range(heads):
        at = pl.ds(h * HD, HD)
        attended[:, at] = (acc[:, at] / totals[h][:, :1]).astype(jnp.bfloat16)

    own = pl.ds(pl.multiple_of(m * cols, cols), cols)

    def peer_of(step):
        return lax.rem(m + step, parts)

    def peer_columns(step):
        return pl.ds(pl.multiple_of(peer_of(step) * cols, cols), cols)

    def proj_copy(step):
        return pltpu.make_async_remote_copy(
            src_ref=proj_send.at[step - 1],
            dst_ref=proj_recv.at[step - 1],
            send_sem=proj_s.at[step - 1],
            recv_sem=proj_r.at[step - 1],
            device_id=(g, peer_of(step)),
            device_id_type=MESH,
        )

    loads[3].wait()
    for step in range(1, parts):
        proj_send[step - 1] = dot(attended[...], out_w[:, peer_columns(step)]).astype(jnp.bfloat16)
        proj_copy(step).start()
    summed = tokens[:, own].astype(jnp.float32) + dot(attended[...], out_w[:, own])
    for step in range(1, parts):
        proj_copy(step).wait_recv()
        summed = summed + proj_recv[step - 1].astype(jnp.float32)
    first[...] = summed.astype(jnp.bfloat16)

    mix[...] = (dot(spread[...], first[...]) / degree[...]).astype(jnp.bfloat16)

    def share(index):
        return pl.ds(pl.multiple_of(index * rows, rows), rows)

    def mix_copy(step):
        peer = lax.rem(g + step, groups)
        return pltpu.make_async_remote_copy(
            src_ref=mix.at[share(peer)],
            dst_ref=got.at[share(g)],
            send_sem=mix_s.at[step],
            recv_sem=mix_r.at[step],
            device_id=(peer, m),
            device_id_type=MESH,
        )

    def mix_start(step, carry):
        mix_copy(step).start()
        return carry

    lax.fori_loop(1, groups, mix_start, 0)
    got[share(g)] = mix[share(g)]

    def back_copy(step):
        peer = lax.rem(g + step, groups)
        return pltpu.make_async_remote_copy(
            src_ref=smooth.at[share(peer)],
            dst_ref=back.at[share(g)],
            send_sem=back_s.at[step],
            recv_sem=back_r.at[step],
            device_id=(peer, m),
            device_id_type=MESH,
        )

    retain = jnp.exp(-decay[...])
    inject = jnp.sqrt(1.0 - retain * retain)

    def advance(index, state):
        @pl.when(index != g)
        def _():
            step = lax.rem(g - index + groups, groups)
            pltpu.make_async_remote_copy(
                src_ref=mix.at[share(index)],
                dst_ref=got.at[share(index)],
                send_sem=mix_s.at[step],
                recv_sem=mix_r.at[step],
                device_id=(index, m),
                device_id_type=MESH,
            ).wait_recv()

        frames = got[share(index)].astype(jnp.float32)
        early = retain * state + inject * frames[:slot]
        late = retain * early + inject * frames[slot:]
        smooth[share(index)] = jnp.concatenate([early, late], axis=0).astype(jnp.bfloat16)

        @pl.when(index != g)
        def _():
            back_copy(lax.rem(index - g + groups, groups)).start()

        return late

    lax.fori_loop(0, groups, advance, jnp.zeros((slot, cols), jnp.float32))
    back[share(g)] = smooth[share(g)]

    def back_wait(step, carry):
        source = lax.rem(g - step + groups, groups)
        pltpu.make_async_remote_copy(
            src_ref=smooth.at[share(source)],
            dst_ref=back.at[share(source)],
            send_sem=back_s.at[step],
            recv_sem=back_r.at[step],
            device_id=(source, m),
            device_id_type=MESH,
        ).wait_recv()
        return carry

    lax.fori_loop(1, groups, back_wait, 0)

    second[m] = (first[...].astype(jnp.float32) + dot(gather[...], back[...])).astype(jnp.bfloat16)

    def second_copy(step, slot_of):
        return pltpu.make_async_remote_copy(
            src_ref=second.at[m],
            dst_ref=second.at[slot_of],
            send_sem=sec_s.at[step - 1],
            recv_sem=sec_r.at[step - 1],
            device_id=(g, peer_of(step)),
            device_id_type=MESH,
        )

    for step in range(1, parts):
        second_copy(step, m).start()
    for step in range(1, parts):
        second_copy(step, lax.rem(m - step + parts, parts)).wait_recv()

    square = 0.0
    for j in range(parts):
        wide = second[j].astype(jnp.float32)
        square = square + jnp.sum(wide * wide, axis=-1, keepdims=True)
    factor = lax.rsqrt(square * (1.0 / (parts * cols)) + 1e-05)
    for j in range(parts):
        at = pl.ds(j * cols, cols)
        normed[:, at] = (second[j].astype(jnp.float32) * factor * gain2[:, at]).astype(jnp.bfloat16)

    tile = min(512, units)
    loads[4].wait()

    def expand(index, carry):
        at = pl.ds(pl.multiple_of(index * tile, tile), tile)
        hidden[:, at] = jax.nn.gelu(dot(normed[...], up_w[:, at]), approximate=True).astype(
            jnp.bfloat16
        )
        return carry

    lax.fori_loop(0, units // tile, expand, 0)

    def ff_copy(step):
        return pltpu.make_async_remote_copy(
            src_ref=ff_send.at[step - 1],
            dst_ref=ff_recv.at[step - 1],
            send_sem=ff_s.at[step - 1],
            recv_sem=ff_r.at[step - 1],
            device_id=(g, peer_of(step)),
            device_id_type=MESH,
        )

    loads[5].wait()
    for step in range(1, parts):
        ff_send[step - 1] = dot(hidden[...], down_w[:, peer_columns(step)]).astype(jnp.bfloat16)
        ff_copy(step).start()
    summed = second[m].astype(jnp.float32) + dot(hidden[...], down_w[:, own])
    for step in range(1, parts):
        ff_copy(step).wait_recv()
        summed = summed + ff_recv[step - 1].astype(jnp.float32)
    out[...] = summed.astype(jnp.bfloat16)

    for i, span in enumerate(spans):

        @pl.when(g + span < groups)
        def _(i=i):
            far_copy(i).wait_send()

    for step in range(1, parts):
        proj_copy(step).wait_send()
        second_copy(step, m).wait_send()
        ff_copy(step).wait_send()

    def drain(step, carry):
        mix_copy(step).wait_send()
        back_copy(step).wait_send()
        return carry

    lax.fori_loop(1, groups, drain, 0)


def per_device(
    tokens,
    norm1_gain,
    query_weight,
    key_weight,
    value_weight,
    output_weight,
    pattern,
    adjacency,
    decay_rate,
    norm2_gain,
    up_weight,
    down_weight,
):
    groups = lax.axis_size("tm")
    parts = lax.axis_size("mp")
    count, features = tokens.shape
    width = query_weight.shape[1]
    sites = adjacency.shape[0]
    steps = count // sites
    assert steps == 2
    cols = features // parts
    units = up_weight.shape[1]
    spans = [1 << k for k in range(pattern.shape[1] - 2) if 1 << k < groups]
    far = len(spans) - 1
    each = sites // groups
    slot = max(8, each)
    rows = steps * slot
    bf16, f32 = jnp.bfloat16, jnp.float32

    links = jnp.maximum(adjacency, jnp.eye(sites, dtype=jnp.int32))
    degree = jnp.sum(links, axis=1).astype(f32)
    lines = jnp.pad(links.reshape(groups, each, sites), ((0, 0), (0, slot - each), (0, 0)))
    step_eye = np.eye(steps, dtype=np.int32)[None, :, None, :, None]
    spread = (
        (lines[:, None, :, None, :] * step_eye).reshape(groups * rows, steps * sites).astype(bf16)
    )
    degree = jnp.pad(degree.reshape(groups, 1, each), ((0, 0), (0, 0), (0, slot - each)), constant_values=1.0)
    degree = jnp.broadcast_to(degree, (groups, steps, slot)).reshape(groups * rows, 1)
    place = np.zeros((steps, sites, groups, steps, slot), np.float32)
    for site in range(sites):
        for step in range(steps):
            place[step, site, site // each, step, site % each] = 1.0
    gather = jnp.asarray(place.reshape(count, groups * rows), bf16)

    vmem = pl.BlockSpec(memory_space=pltpu.VMEM)
    smem = pl.BlockSpec(memory_space=pltpu.SMEM)
    hbm = pl.BlockSpec(memory_space=pl.ANY)
    others = max(1, parts - 1)
    dma = pltpu.SemaphoreType.DMA
    return pl.pallas_call(
        functools.partial(kernel, groups, parts, spans, rows, slot),
        out_shape=jax.ShapeDtypeStruct((count, cols), bf16),
        in_specs=[vmem, vmem, smem] + [vmem] * 5 + [hbm] * 6,
        out_specs=vmem,
        scratch_shapes=[
            pltpu.VMEM((features, 3 * width), bf16),
            pltpu.VMEM((width, features), bf16),
            pltpu.VMEM((features, units), bf16),
            pltpu.VMEM((units, features), bf16),
            pltpu.VMEM((count, features), bf16),
            pltpu.VMEM((count, width), bf16),
            pltpu.VMEM((4 + far, sites, 2 * width), bf16),
            pltpu.VMEM((max(1, far), sites, 2 * width), bf16),
            pltpu.VMEM((width // HD, count, HD), f32),
            pltpu.VMEM((width // HD, count, HD), f32),
            pltpu.VMEM((count, width), f32),
            pltpu.VMEM((count, width), bf16),
            pltpu.VMEM((others, count, cols), bf16),
            pltpu.VMEM((others, count, cols), bf16),
            pltpu.VMEM((count, cols), bf16),
            pltpu.VMEM((groups * rows, cols), bf16),
            pltpu.VMEM((groups * rows, cols), bf16),
            pltpu.VMEM((groups * rows, cols), bf16),
            pltpu.VMEM((groups * rows, cols), bf16),
            pltpu.VMEM((parts, count, cols), bf16),
            pltpu.VMEM((count, units), bf16),
            pltpu.VMEM((others, count, cols), bf16),
            pltpu.VMEM((others, count, cols), bf16),
            dma((6,)),
            dma((len(spans),)),
            dma((len(spans),)),
            dma((others,)),
            dma((others,)),
            dma((groups,)),
            dma((groups,)),
            dma((groups,)),
            dma((groups,)),
            dma((others,)),
            dma((others,)),
            dma((others,)),
            dma((others,)),
        ],
        compiler_params=pltpu.CompilerParams(
            collective_id=0, has_side_effects=True, vmem_limit_bytes=48 * 1024 * 1024
        ),
    )(
        tokens,
        norm1_gain.reshape(1, -1),
        pattern,
        decay_rate.reshape(1, -1),
        norm2_gain.reshape(1, -1),
        spread,
        degree,
        gather,
        query_weight,
        key_weight,
        value_weight,
        output_weight,
        up_weight,
        down_weight,
    )


def solution(mesh):
    placed = (
        P("tm", None),
        P(),
        P(None, "mp"),
        P(None, "mp"),
        P(None, "mp"),
        P("mp", None),
        P(),
        P(),
        P("mp"),
        P(),
        P(None, "mp"),
        P("mp", None),
    )
    return jax.shard_map(
        per_device, mesh=mesh, in_specs=placed, out_specs=P("tm", "mp"), check_vma=False
    )
```

```python
import functools
import math

import jax
import jax.numpy as jnp
from jax import lax
from jax.experimental import pallas as pl
from jax.experimental.pallas import tpu as pltpu
from jax.sharding import PartitionSpec as P

HD = 128
MESH = pl.DeviceIdType.MESH


def dot(a, b):
    return jnp.dot(a, b, preferred_element_type=jnp.float32)


def kernel(
    groups,
    parts,
    spans,
    rows,
    slot,
    pattern,
    tokens_in,
    gain1_in,
    gain2_in,
    decay_in,
    adjacency_in,
    wq,
    wk,
    wv,
    wo,
    wu,
    wd,
    out,
    tokens,
    gain1,
    gain2,
    decay,
    adjacency,
    spread,
    gather,
    qkv_w,
    out_w,
    up_w,
    down_w,
    normed,
    queries,
    kv,
    sel,
    tops,
    totals,
    acc,
    attended,
    proj_send,
    proj_recv,
    first,
    mix,
    got,
    smooth,
    back,
    second,
    hidden,
    ff_send,
    ff_recv,
    in_sem,
    w_sem,
    far_s,
    far_r,
    proj_s,
    proj_r,
    mix_s,
    mix_r,
    back_s,
    back_r,
    sec_s,
    sec_r,
    ff_s,
    ff_r,
):
    g = lax.axis_index("tm")
    m = lax.axis_index("mp")
    sites = kv.shape[1]
    width = kv.shape[2] // 2
    heads = width // HD
    cols = out.shape[1]
    units = hidden.shape[1]

    inputs = [
        pltpu.make_async_copy(tokens_in, tokens, in_sem.at[0]),
        pltpu.make_async_copy(gain1_in, gain1, in_sem.at[1]),
        pltpu.make_async_copy(gain2_in, gain2, in_sem.at[2]),
        pltpu.make_async_copy(decay_in, decay, in_sem.at[3]),
        pltpu.make_async_copy(adjacency_in, adjacency, in_sem.at[4]),
    ]
    for load in inputs:
        load.start()
    loads = [
        pltpu.make_async_copy(wk, qkv_w.at[:, pl.ds(0, width)], w_sem.at[0]),
        pltpu.make_async_copy(wv, qkv_w.at[:, pl.ds(width, width)], w_sem.at[1]),
        pltpu.make_async_copy(wq, qkv_w.at[:, pl.ds(2 * width, width)], w_sem.at[2]),
        pltpu.make_async_copy(wo, out_w, w_sem.at[3]),
        pltpu.make_async_copy(wu, up_w, w_sem.at[4]),
        pltpu.make_async_copy(wd, down_w, w_sem.at[5]),
    ]
    for load in loads:
        load.start()

    barrier = pltpu.get_barrier_semaphore()

    def greet(step, carry):
        pl.semaphore_signal(
            barrier, inc=1, device_id=(lax.rem(g + step, groups), m), device_id_type=MESH
        )
        return carry

    lax.fori_loop(1, groups, greet, 0)
    for step in range(1, parts):
        pl.semaphore_signal(
            barrier, inc=1, device_id=(g, lax.rem(m + step, parts)), device_id_type=MESH
        )

    for load in inputs:
        load.wait()
    wide = tokens[...].astype(jnp.float32)
    square = jnp.mean(wide * wide, axis=-1, keepdims=True)
    normed[...] = (wide * lax.rsqrt(square + 1e-05) * gain1[...]).astype(jnp.bfloat16)

    for j in range(2):
        loads[j].wait()
        product = dot(normed[...], qkv_w[:, pl.ds(j * width, width)]).astype(jnp.bfloat16)
        kv[0, :, pl.ds(j * width, width)] = product[:sites]
        kv[1, :, pl.ds(j * width, width)] = product[sites:]
    for i, span in enumerate(spans[1:]):
        target = jnp.minimum(g + span, groups - 1)
        pick = lax.rem(jnp.maximum(pattern[3 + i, 2 * target], 0), 2).astype(jnp.float32)
        sel[i] = (
            kv[0].astype(jnp.float32) * (1.0 - pick) + kv[1].astype(jnp.float32) * pick
        ).astype(jnp.bfloat16)

    pl.semaphore_wait(barrier, groups + parts - 2)

    def far_copy(i):
        source = kv.at[pl.ds(0, 2)] if i == 0 else sel.at[pl.ds(i - 1, 1)]
        target = kv.at[pl.ds(2, 2)] if i == 0 else kv.at[pl.ds(3 + i, 1)]
        return pltpu.make_async_remote_copy(
            src_ref=source,
            dst_ref=target,
            send_sem=far_s.at[i],
            recv_sem=far_r.at[i],
            device_id=(jnp.minimum(g + spans[i], groups - 1), m),
            device_id_type=MESH,
        )

    for i in reversed(range(len(spans))):

        @pl.when(g + spans[i] < groups)
        def _(i=i):
            far_copy(i).start()

    loads[2].wait()
    queries[...] = dot(normed[...], qkv_w[:, pl.ds(2 * width, width)]).astype(jnp.bfloat16)

    each = sites // groups
    line = lax.broadcasted_iota(jnp.int32, adjacency.shape, 0)
    other = lax.broadcasted_iota(jnp.int32, adjacency.shape, 1)
    links = jnp.where(line == other, 1, adjacency[...]).astype(jnp.float32).astype(jnp.bfloat16)
    for step in range(2):
        packed = lax.broadcasted_iota(jnp.int32, (groups * rows, sites), 0)
        site = lax.broadcasted_iota(jnp.int32, (groups * rows, sites), 1)
        inner = packed % rows
        spot = inner % slot
        here = (inner // slot == step) & (spot < each) & (packed // rows * each + spot == site)
        spread[:, pl.ds(step * sites, sites)] = dot(
            jnp.where(here, 1.0, 0.0).astype(jnp.bfloat16), links
        ).astype(jnp.bfloat16)
        site = lax.broadcasted_iota(jnp.int32, (sites, groups * rows), 0)
        packed = lax.broadcasted_iota(jnp.int32, (sites, groups * rows), 1)
        inner = packed % rows
        spot = inner % slot
        here = (inner // slot == step) & (spot < each) & (packed // rows * each + spot == site)
        gather[pl.ds(step * sites, sites), :] = jnp.where(here, 1.0, 0.0).astype(jnp.bfloat16)
    degree = jnp.maximum(
        jnp.sum(spread[...].astype(jnp.float32), axis=-1, keepdims=True), 1.0
    )

    scale = 1.0 / math.sqrt(HD)

    def attend(start, count, hide, fresh):
        for h in range(heads):
            at = pl.ds(h * HD, HD)
            keys = kv[pl.ds(start, count), :, at].reshape(count * sites, HD)
            values = kv[pl.ds(start, count), :, pl.ds(width + h * HD, HD)].reshape(
                count * sites, HD
            )
            scores = (
                lax.dot_general(
                    queries[:, at],
                    keys,
                    (((1,), (1,)), ((), ())),
                    preferred_element_type=jnp.float32,
                )
                * scale
            )
            if hide is not None:
                step = lax.broadcasted_iota(jnp.int32, scores.shape, 0) // sites
                block = lax.broadcasted_iota(jnp.int32, scores.shape, 1) // sites
                scores = jnp.where((step == hide[0]) & (block == hide[1]), -jnp.inf, scores)
            top = jnp.max(scores, axis=-1, keepdims=True)
            if fresh:
                probs = jnp.exp(scores - top)
                total = jnp.sum(probs, axis=-1, keepdims=True)
                part = dot(probs.astype(jnp.bfloat16), values)
            else:
                old = tops[h][:, :1]
                top = jnp.maximum(top, old)
                factor = jnp.exp(old - top)
                probs = jnp.exp(scores - top)
                total = totals[h][:, :1] * factor + jnp.sum(probs, axis=-1, keepdims=True)
                part = acc[:, at] * factor + dot(probs.astype(jnp.bfloat16), values)
            tops[h] = jnp.broadcast_to(top, tops.shape[1:])
            totals[h] = jnp.broadcast_to(total, totals.shape[1:])
            acc[:, at] = part

    attend(0, 2, (0, 1), True)
    for i, span in enumerate(spans):

        @pl.when(g >= span)
        def _(i=i):
            far_copy(i).wait_recv()
            if i == 0:
                attend(2, 2, (1, 1), False)
            else:
                attend(3 + i, 1, None, False)

    for h in range(heads):
        at = pl.ds(h * HD, HD)
        attended[:, at] = (acc[:, at] / totals[h][:, :1]).astype(jnp.bfloat16)

    own = pl.ds(pl.multiple_of(m * cols, cols), cols)

    def peer_of(step):
        return lax.rem(m + step, parts)

    def peer_columns(step):
        return pl.ds(pl.multiple_of(peer_of(step) * cols, cols), cols)

    def proj_copy(step):
        return pltpu.make_async_remote_copy(
            src_ref=proj_send.at[step - 1],
            dst_ref=proj_recv.at[step - 1],
            send_sem=proj_s.at[step - 1],
            recv_sem=proj_r.at[step - 1],
            device_id=(g, peer_of(step)),
            device_id_type=MESH,
        )

    loads[3].wait()
    for step in range(1, parts):
        proj_send[step - 1] = dot(attended[...], out_w[:, peer_columns(step)]).astype(jnp.bfloat16)
        proj_copy(step).start()
    summed = tokens[:, own].astype(jnp.float32) + dot(attended[...], out_w[:, own])
    for step in range(1, parts):
        proj_copy(step).wait_recv()
        summed = summed + proj_recv[step - 1].astype(jnp.float32)
    first[...] = summed.astype(jnp.bfloat16)

    mix[...] = (dot(spread[...], first[...]) / degree).astype(jnp.bfloat16)

    def share(index):
        return pl.ds(pl.multiple_of(index * rows, rows), rows)

    def mix_copy(step):
        peer = lax.rem(g + step, groups)
        return pltpu.make_async_remote_copy(
            src_ref=mix.at[share(peer)],
            dst_ref=got.at[share(g)],
            send_sem=mix_s.at[step],
            recv_sem=mix_r.at[step],
            device_id=(peer, m),
            device_id_type=MESH,
        )

    def mix_start(step, carry):
        mix_copy(step).start()
        return carry

    lax.fori_loop(1, groups, mix_start, 0)
    got[share(g)] = mix[share(g)]

    def back_copy(step):
        peer = lax.rem(g + step, groups)
        return pltpu.make_async_remote_copy(
            src_ref=smooth.at[share(peer)],
            dst_ref=back.at[share(g)],
            send_sem=back_s.at[step],
            recv_sem=back_r.at[step],
            device_id=(peer, m),
            device_id_type=MESH,
        )

    retain = jnp.exp(-decay[...])
    inject = jnp.sqrt(1.0 - retain * retain)

    def advance(index, state):
        @pl.when(index != g)
        def _():
            step = lax.rem(g - index + groups, groups)
            pltpu.make_async_remote_copy(
                src_ref=mix.at[share(index)],
                dst_ref=got.at[share(index)],
                send_sem=mix_s.at[step],
                recv_sem=mix_r.at[step],
                device_id=(index, m),
                device_id_type=MESH,
            ).wait_recv()

        frames = got[share(index)].astype(jnp.float32)
        early = retain * state + inject * frames[:slot]
        late = retain * early + inject * frames[slot:]
        smooth[share(index)] = jnp.concatenate([early, late], axis=0).astype(jnp.bfloat16)

        @pl.when(index != g)
        def _():
            back_copy(lax.rem(index - g + groups, groups)).start()

        return late

    lax.fori_loop(0, groups, advance, jnp.zeros((slot, cols), jnp.float32))
    back[share(g)] = smooth[share(g)]

    def back_wait(step, carry):
        source = lax.rem(g - step + groups, groups)
        pltpu.make_async_remote_copy(
            src_ref=smooth.at[share(source)],
            dst_ref=back.at[share(source)],
            send_sem=back_s.at[step],
            recv_sem=back_r.at[step],
            device_id=(source, m),
            device_id_type=MESH,
        ).wait_recv()
        return carry

    lax.fori_loop(1, groups, back_wait, 0)

    second[m] = (first[...].astype(jnp.float32) + dot(gather[...], back[...])).astype(jnp.bfloat16)

    def second_copy(step, slot_of):
        return pltpu.make_async_remote_copy(
            src_ref=second.at[m],
            dst_ref=second.at[slot_of],
            send_sem=sec_s.at[step - 1],
            recv_sem=sec_r.at[step - 1],
            device_id=(g, peer_of(step)),
            device_id_type=MESH,
        )

    for step in range(1, parts):
        second_copy(step, m).start()
    for step in range(1, parts):
        second_copy(step, lax.rem(m - step + parts, parts)).wait_recv()

    square = 0.0
    for j in range(parts):
        wide = second[j].astype(jnp.float32)
        square = square + jnp.sum(wide * wide, axis=-1, keepdims=True)
    factor = lax.rsqrt(square * (1.0 / (parts * cols)) + 1e-05)
    for j in range(parts):
        at = pl.ds(j * cols, cols)
        normed[:, at] = (second[j].astype(jnp.float32) * factor * gain2[:, at]).astype(jnp.bfloat16)

    tile = min(512, units)
    loads[4].wait()

    def expand(index, carry):
        at = pl.ds(pl.multiple_of(index * tile, tile), tile)
        hidden[:, at] = jax.nn.gelu(dot(normed[...], up_w[:, at]), approximate=True).astype(
            jnp.bfloat16
        )
        return carry

    lax.fori_loop(0, units // tile, expand, 0)

    def ff_copy(step):
        return pltpu.make_async_remote_copy(
            src_ref=ff_send.at[step - 1],
            dst_ref=ff_recv.at[step - 1],
            send_sem=ff_s.at[step - 1],
            recv_sem=ff_r.at[step - 1],
            device_id=(g, peer_of(step)),
            device_id_type=MESH,
        )

    loads[5].wait()
    for step in range(1, parts):
        ff_send[step - 1] = dot(hidden[...], down_w[:, peer_columns(step)]).astype(jnp.bfloat16)
        ff_copy(step).start()
    summed = second[m].astype(jnp.float32) + dot(hidden[...], down_w[:, own])
    for step in range(1, parts):
        ff_copy(step).wait_recv()
        summed = summed + ff_recv[step - 1].astype(jnp.float32)
    out[...] = summed.astype(jnp.bfloat16)

    for i, span in enumerate(spans):

        @pl.when(g + span < groups)
        def _(i=i):
            far_copy(i).wait_send()

    for step in range(1, parts):
        proj_copy(step).wait_send()
        second_copy(step, m).wait_send()
        ff_copy(step).wait_send()

    def drain(step, carry):
        mix_copy(step).wait_send()
        back_copy(step).wait_send()
        return carry

    lax.fori_loop(1, groups, drain, 0)


def per_device(
    tokens,
    norm1_gain,
    query_weight,
    key_weight,
    value_weight,
    output_weight,
    pattern,
    adjacency,
    decay_rate,
    norm2_gain,
    up_weight,
    down_weight,
):
    groups = lax.axis_size("tm")
    parts = lax.axis_size("mp")
    count, features = tokens.shape
    width = query_weight.shape[1]
    sites = adjacency.shape[0]
    steps = count // sites
    assert steps == 2
    cols = features // parts
    units = up_weight.shape[1]
    spans = [1 << k for k in range(pattern.shape[1] - 2) if 1 << k < groups]
    far = len(spans) - 1
    each = sites // groups
    slot = max(8, each)
    rows = steps * slot
    bf16, f32 = jnp.bfloat16, jnp.float32

    vmem = pl.BlockSpec(memory_space=pltpu.VMEM)
    smem = pl.BlockSpec(memory_space=pltpu.SMEM)
    hbm = pl.BlockSpec(memory_space=pl.ANY)
    others = max(1, parts - 1)
    dma = pltpu.SemaphoreType.DMA
    return pl.pallas_call(
        functools.partial(kernel, groups, parts, spans, rows, slot),
        out_shape=jax.ShapeDtypeStruct((count, cols), bf16),
        in_specs=[smem] + [hbm] * 11,
        out_specs=vmem,
        scratch_shapes=[
            pltpu.VMEM((count, features), bf16),
            pltpu.VMEM((1, features), f32),
            pltpu.VMEM((1, features), f32),
            pltpu.VMEM((1, cols), f32),
            pltpu.VMEM((sites, sites), jnp.int32),
            pltpu.VMEM((groups * rows, count), bf16),
            pltpu.VMEM((count, groups * rows), bf16),
            pltpu.VMEM((features, 3 * width), bf16),
            pltpu.VMEM((width, features), bf16),
            pltpu.VMEM((features, units), bf16),
            pltpu.VMEM((units, features), bf16),
            pltpu.VMEM((count, features), bf16),
            pltpu.VMEM((count, width), bf16),
            pltpu.VMEM((4 + far, sites, 2 * width), bf16),
            pltpu.VMEM((max(1, far), sites, 2 * width), bf16),
            pltpu.VMEM((width // HD, count, HD), f32),
            pltpu.VMEM((width // HD, count, HD), f32),
            pltpu.VMEM((count, width), f32),
            pltpu.VMEM((count, width), bf16),
            pltpu.VMEM((others, count, cols), bf16),
            pltpu.VMEM((others, count, cols), bf16),
            pltpu.VMEM((count, cols), bf16),
            pltpu.VMEM((groups * rows, cols), bf16),
            pltpu.VMEM((groups * rows, cols), bf16),
            pltpu.VMEM((groups * rows, cols), bf16),
            pltpu.VMEM((groups * rows, cols), bf16),
            pltpu.VMEM((parts, count, cols), bf16),
            pltpu.VMEM((count, units), bf16),
            pltpu.VMEM((others, count, cols), bf16),
            pltpu.VMEM((others, count, cols), bf16),
            dma((5,)),
            dma((6,)),
            dma((len(spans),)),
            dma((len(spans),)),
            dma((others,)),
            dma((others,)),
            dma((groups,)),
            dma((groups,)),
            dma((groups,)),
            dma((groups,)),
            dma((others,)),
            dma((others,)),
            dma((others,)),
            dma((others,)),
        ],
        compiler_params=pltpu.CompilerParams(
            collective_id=0, has_side_effects=True, vmem_limit_bytes=60 * 1024 * 1024
        ),
    )(
        pattern.T,
        tokens,
        norm1_gain.reshape(1, -1),
        norm2_gain.reshape(1, -1),
        decay_rate.reshape(1, -1),
        adjacency,
        query_weight,
        key_weight,
        value_weight,
        output_weight,
        up_weight,
        down_weight,
    )


def solution(mesh):
    placed = (
        P("tm", None),
        P(),
        P(None, "mp"),
        P(None, "mp"),
        P(None, "mp"),
        P("mp", None),
        P(),
        P(),
        P("mp"),
        P(),
        P(None, "mp"),
        P("mp", None),
    )
    return jax.shard_map(
        per_device, mesh=mesh, in_specs=placed, out_specs=P("tm", "mp"), check_vma=False
    )
```

```python
import functools
import math

import jax
import jax.numpy as jnp
from jax import lax
from jax.experimental import pallas as pl
from jax.experimental.pallas import tpu as pltpu
from jax.sharding import PartitionSpec as P

HD = 128
MESH = pl.DeviceIdType.MESH


def dot(a, b):
    return jnp.dot(a, b, preferred_element_type=jnp.float32)


def kernel(
    groups,
    parts,
    spans,
    rows,
    slot,
    pattern,
    tokens_in,
    gain1_in,
    gain2_in,
    decay_in,
    adjacency_in,
    wq,
    wk,
    wv,
    wo,
    wu,
    wd,
    out,
    tokens,
    gain1,
    gain2,
    decay,
    adjacency,
    spread,
    gather,
    qkv_w,
    out_w,
    up_w,
    down_w,
    normed,
    queries,
    kv,
    shared,
    far,
    sel,
    tops,
    totals,
    acc,
    attended,
    proj_send,
    proj_recv,
    first,
    mix,
    got,
    smooth,
    back,
    second,
    hidden,
    ff_send,
    ff_recv,
    in_sem,
    w_sem,
    far_s,
    far_r,
    pass_s,
    pass_r,
    proj_s,
    proj_r,
    mix_s,
    mix_r,
    back_s,
    back_r,
    sec_s,
    sec_r,
    ff_s,
    ff_r,
):
    g = lax.axis_index("tm")
    m = lax.axis_index("mp")
    sites = kv.shape[1]
    width = kv.shape[2] // 2
    heads = width // HD
    cols = out.shape[1]
    units = hidden.shape[1]

    inputs = [
        pltpu.make_async_copy(tokens_in, tokens, in_sem.at[0]),
        pltpu.make_async_copy(gain1_in, gain1, in_sem.at[1]),
        pltpu.make_async_copy(gain2_in, gain2, in_sem.at[2]),
        pltpu.make_async_copy(decay_in, decay, in_sem.at[3]),
        pltpu.make_async_copy(adjacency_in, adjacency, in_sem.at[4]),
    ]
    for load in inputs:
        load.start()
    loads = [
        pltpu.make_async_copy(wk, qkv_w.at[:, pl.ds(0, width)], w_sem.at[0]),
        pltpu.make_async_copy(wv, qkv_w.at[:, pl.ds(width, width)], w_sem.at[1]),
        pltpu.make_async_copy(wq, qkv_w.at[:, pl.ds(2 * width, width)], w_sem.at[2]),
        pltpu.make_async_copy(wo, out_w, w_sem.at[3]),
        pltpu.make_async_copy(wu, up_w, w_sem.at[4]),
        pltpu.make_async_copy(wd, down_w, w_sem.at[5]),
    ]
    for load in loads:
        load.start()

    barrier = pltpu.get_barrier_semaphore()

    def greet(step, carry):
        pl.semaphore_signal(
            barrier, inc=1, device_id=(lax.rem(g + step, groups), m), device_id_type=MESH
        )
        return carry

    lax.fori_loop(1, groups, greet, 0)
    for step in range(1, parts):
        pl.semaphore_signal(
            barrier, inc=1, device_id=(g, lax.rem(m + step, parts)), device_id_type=MESH
        )

    for load in inputs:
        load.wait()
    own = pl.ds(pl.multiple_of(m * cols, cols), cols)
    shared[...] = tokens[:, own]
    for i, span in enumerate(spans[1:]):
        target = jnp.minimum(g + span, groups - 1)
        pick = lax.rem(jnp.maximum(pattern[3 + i, 2 * target], 0), 2).astype(jnp.float32)
        sel[i] = (
            shared[:sites].astype(jnp.float32) * (1.0 - pick)
            + shared[sites:].astype(jnp.float32) * pick
        ).astype(jnp.bfloat16)

    def peer_of(step):
        return lax.rem(m + step, parts)

    def far_rows(i):
        return pl.ds(0, 2 * sites) if i == 0 else pl.ds((1 + i) * sites, sites)

    def far_copy(i):
        return pltpu.make_async_remote_copy(
            src_ref=shared if i == 0 else sel.at[i - 1],
            dst_ref=far.at[m, far_rows(i)],
            send_sem=far_s.at[i],
            recv_sem=far_r.at[i],
            device_id=(jnp.minimum(g + spans[i], groups - 1), m),
            device_id_type=MESH,
        )

    def pass_copy(i, step, part):
        return pltpu.make_async_remote_copy(
            src_ref=far.at[m, far_rows(i)],
            dst_ref=far.at[part, far_rows(i)],
            send_sem=pass_s.at[i, step - 1],
            recv_sem=pass_r.at[i, step - 1],
            device_id=(g, peer_of(step)),
            device_id_type=MESH,
        )

    pl.semaphore_wait(barrier, groups + parts - 2)
    for i in reversed(range(len(spans))):

        @pl.when(g + spans[i] < groups)
        def _(i=i):
            far_copy(i).start()

    wide = tokens[...].astype(jnp.float32)
    square = jnp.mean(wide * wide, axis=-1, keepdims=True)
    normed[...] = (wide * lax.rsqrt(square + 1e-05) * gain1[...]).astype(jnp.bfloat16)

    for j in range(2):
        loads[j].wait()
        product = dot(normed[...], qkv_w[:, pl.ds(j * width, width)]).astype(jnp.bfloat16)
        kv[0, :, pl.ds(j * width, width)] = product[:sites]
        kv[1, :, pl.ds(j * width, width)] = product[sites:]
    loads[2].wait()
    queries[...] = dot(normed[...], qkv_w[:, pl.ds(2 * width, width)]).astype(jnp.bfloat16)

    each = sites // groups
    line = lax.broadcasted_iota(jnp.int32, adjacency.shape, 0)
    other = lax.broadcasted_iota(jnp.int32, adjacency.shape, 1)
    links = jnp.where(line == other, 1, adjacency[...]).astype(jnp.float32).astype(jnp.bfloat16)
    for step in range(2):
        packed = lax.broadcasted_iota(jnp.int32, (groups * rows, sites), 0)
        site = lax.broadcasted_iota(jnp.int32, (groups * rows, sites), 1)
        inner = packed % rows
        spot = inner % slot
        here = (inner // slot == step) & (spot < each) & (packed // rows * each + spot == site)
        spread[:, pl.ds(step * sites, sites)] = dot(
            jnp.where(here, 1.0, 0.0).astype(jnp.bfloat16), links
        ).astype(jnp.bfloat16)
        site = lax.broadcasted_iota(jnp.int32, (sites, groups * rows), 0)
        packed = lax.broadcasted_iota(jnp.int32, (sites, groups * rows), 1)
        inner = packed % rows
        spot = inner % slot
        here = (inner // slot == step) & (spot < each) & (packed // rows * each + spot == site)
        gather[pl.ds(step * sites, sites), :] = jnp.where(here, 1.0, 0.0).astype(jnp.bfloat16)
    degree = jnp.maximum(
        jnp.sum(spread[...].astype(jnp.float32), axis=-1, keepdims=True), 1.0
    )

    scale = 1.0 / math.sqrt(HD)

    def attend(start, count, hide, fresh):
        for h in range(heads):
            at = pl.ds(h * HD, HD)
            keys = kv[pl.ds(start, count), :, at].reshape(count * sites, HD)
            values = kv[pl.ds(start, count), :, pl.ds(width + h * HD, HD)].reshape(
                count * sites, HD
            )
            scores = (
                lax.dot_general(
                    queries[:, at],
                    keys,
                    (((1,), (1,)), ((), ())),
                    preferred_element_type=jnp.float32,
                )
                * scale
            )
            if hide is not None:
                step = lax.broadcasted_iota(jnp.int32, scores.shape, 0) // sites
                block = lax.broadcasted_iota(jnp.int32, scores.shape, 1) // sites
                scores = jnp.where((step == hide[0]) & (block == hide[1]), -jnp.inf, scores)
            top = jnp.max(scores, axis=-1, keepdims=True)
            if fresh:
                probs = jnp.exp(scores - top)
                total = jnp.sum(probs, axis=-1, keepdims=True)
                part = dot(probs.astype(jnp.bfloat16), values)
            else:
                old = tops[h][:, :1]
                top = jnp.maximum(top, old)
                factor = jnp.exp(old - top)
                probs = jnp.exp(scores - top)
                total = totals[h][:, :1] * factor + jnp.sum(probs, axis=-1, keepdims=True)
                part = acc[:, at] * factor + dot(probs.astype(jnp.bfloat16), values)
            tops[h] = jnp.broadcast_to(top, tops.shape[1:])
            totals[h] = jnp.broadcast_to(total, totals.shape[1:])
            acc[:, at] = part

    def hand_on(i):
        @pl.when(g >= spans[i])
        def _():
            far_copy(i).wait_recv()
            for step in range(1, parts):
                pass_copy(i, step, m).start()

    def absorb(i):
        at_rows = far_rows(i)
        blocks = 2 if i == 0 else 1
        start = 2 if i == 0 else 3 + i

        @pl.when(g >= spans[i])
        def _():
            for step in range(1, parts):
                pass_copy(i, step, lax.rem(m - step + parts, parts)).wait_recv()
            square = 0.0
            for j in range(parts):
                wide = far[j, at_rows].astype(jnp.float32)
                square = square + jnp.sum(wide * wide, axis=-1, keepdims=True)
            factor = lax.rsqrt(square * (1.0 / (parts * cols)) + 1e-05)
            count = blocks * sites
            for j in range(parts):
                at = pl.ds(j * cols, cols)
                normed[pl.ds(0, count), at] = (
                    far[j, at_rows].astype(jnp.float32) * factor * gain1[:, at]
                ).astype(jnp.bfloat16)
            for j in range(2):
                at = pl.ds(j * width, width)
                product = dot(normed[pl.ds(0, count), :], qkv_w[:, at]).astype(jnp.bfloat16)
                for block in range(blocks):
                    kv[start + block, :, at] = product[block * sites : (block + 1) * sites]
            attend(start, blocks, (1, 1) if i == 0 else None, False)

    hand_on(0)
    attend(0, 2, (0, 1), True)
    for i in range(1, len(spans)):
        hand_on(i)
        absorb(i - 1)
    absorb(len(spans) - 1)

    for h in range(heads):
        at = pl.ds(h * HD, HD)
        attended[:, at] = (acc[:, at] / totals[h][:, :1]).astype(jnp.bfloat16)

    def peer_columns(step):
        return pl.ds(pl.multiple_of(peer_of(step) * cols, cols), cols)

    def proj_copy(step):
        return pltpu.make_async_remote_copy(
            src_ref=proj_send.at[step - 1],
            dst_ref=proj_recv.at[step - 1],
            send_sem=proj_s.at[step - 1],
            recv_sem=proj_r.at[step - 1],
            device_id=(g, peer_of(step)),
            device_id_type=MESH,
        )

    loads[3].wait()
    for step in range(1, parts):
        proj_send[step - 1] = dot(attended[...], out_w[:, peer_columns(step)]).astype(jnp.bfloat16)
        proj_copy(step).start()
    summed = shared[...].astype(jnp.float32) + dot(attended[...], out_w[:, own])
    for step in range(1, parts):
        proj_copy(step).wait_recv()
        summed = summed + proj_recv[step - 1].astype(jnp.float32)
    first[...] = summed.astype(jnp.bfloat16)

    mix[...] = (dot(spread[...], first[...]) / degree).astype(jnp.bfloat16)

    def share(index):
        return pl.ds(pl.multiple_of(index * rows, rows), rows)

    def mix_copy(step):
        peer = lax.rem(g + step, groups)
        return pltpu.make_async_remote_copy(
            src_ref=mix.at[share(peer)],
            dst_ref=got.at[share(g)],
            send_sem=mix_s.at[step],
            recv_sem=mix_r.at[step],
            device_id=(peer, m),
            device_id_type=MESH,
        )

    def mix_start(step, carry):
        mix_copy(step).start()
        return carry

    lax.fori_loop(1, groups, mix_start, 0)
    got[share(g)] = mix[share(g)]

    def back_copy(step):
        peer = lax.rem(g + step, groups)
        return pltpu.make_async_remote_copy(
            src_ref=smooth.at[share(peer)],
            dst_ref=back.at[share(g)],
            send_sem=back_s.at[step],
            recv_sem=back_r.at[step],
            device_id=(peer, m),
            device_id_type=MESH,
        )

    retain = jnp.exp(-decay[...])
    inject = jnp.sqrt(1.0 - retain * retain)

    def advance(index, state):
        @pl.when(index != g)
        def _():
            step = lax.rem(g - index + groups, groups)
            pltpu.make_async_remote_copy(
                src_ref=mix.at[share(index)],
                dst_ref=got.at[share(index)],
                send_sem=mix_s.at[step],
                recv_sem=mix_r.at[step],
                device_id=(index, m),
                device_id_type=MESH,
            ).wait_recv()

        frames = got[share(index)].astype(jnp.float32)
        early = retain * state + inject * frames[:slot]
        late = retain * early + inject * frames[slot:]
        smooth[share(index)] = jnp.concatenate([early, late], axis=0).astype(jnp.bfloat16)

        @pl.when(index != g)
        def _():
            back_copy(lax.rem(index - g + groups, groups)).start()

        return late

    lax.fori_loop(0, groups, advance, jnp.zeros((slot, cols), jnp.float32))
    back[share(g)] = smooth[share(g)]

    def back_wait(step, carry):
        source = lax.rem(g - step + groups, groups)
        pltpu.make_async_remote_copy(
            src_ref=smooth.at[share(source)],
            dst_ref=back.at[share(source)],
            send_sem=back_s.at[step],
            recv_sem=back_r.at[step],
            device_id=(source, m),
            device_id_type=MESH,
        ).wait_recv()
        return carry

    lax.fori_loop(1, groups, back_wait, 0)

    second[m] = (first[...].astype(jnp.float32) + dot(gather[...], back[...])).astype(jnp.bfloat16)

    def second_copy(step, slot_of):
        return pltpu.make_async_remote_copy(
            src_ref=second.at[m],
            dst_ref=second.at[slot_of],
            send_sem=sec_s.at[step - 1],
            recv_sem=sec_r.at[step - 1],
            device_id=(g, peer_of(step)),
            device_id_type=MESH,
        )

    for step in range(1, parts):
        second_copy(step, m).start()
    for step in range(1, parts):
        second_copy(step, lax.rem(m - step + parts, parts)).wait_recv()

    square = 0.0
    for j in range(parts):
        wide = second[j].astype(jnp.float32)
        square = square + jnp.sum(wide * wide, axis=-1, keepdims=True)
    factor = lax.rsqrt(square * (1.0 / (parts * cols)) + 1e-05)
    for j in range(parts):
        at = pl.ds(j * cols, cols)
        normed[:, at] = (second[j].astype(jnp.float32) * factor * gain2[:, at]).astype(jnp.bfloat16)

    tile = min(512, units)
    loads[4].wait()

    def expand(index, carry):
        at = pl.ds(pl.multiple_of(index * tile, tile), tile)
        hidden[:, at] = jax.nn.gelu(dot(normed[...], up_w[:, at]), approximate=True).astype(
            jnp.bfloat16
        )
        return carry

    lax.fori_loop(0, units // tile, expand, 0)

    def ff_copy(step):
        return pltpu.make_async_remote_copy(
            src_ref=ff_send.at[step - 1],
            dst_ref=ff_recv.at[step - 1],
            send_sem=ff_s.at[step - 1],
            recv_sem=ff_r.at[step - 1],
            device_id=(g, peer_of(step)),
            device_id_type=MESH,
        )

    loads[5].wait()
    for step in range(1, parts):
        ff_send[step - 1] = dot(hidden[...], down_w[:, peer_columns(step)]).astype(jnp.bfloat16)
        ff_copy(step).start()
    summed = second[m].astype(jnp.float32) + dot(hidden[...], down_w[:, own])
    for step in range(1, parts):
        ff_copy(step).wait_recv()
        summed = summed + ff_recv[step - 1].astype(jnp.float32)
    out[...] = summed.astype(jnp.bfloat16)

    for i, span in enumerate(spans):

        @pl.when(g + span < groups)
        def _(i=i):
            far_copy(i).wait_send()

        @pl.when(g >= span)
        def _(i=i):
            for step in range(1, parts):
                pass_copy(i, step, m).wait_send()

    for step in range(1, parts):
        proj_copy(step).wait_send()
        second_copy(step, m).wait_send()
        ff_copy(step).wait_send()

    def drain(step, carry):
        mix_copy(step).wait_send()
        back_copy(step).wait_send()
        return carry

    lax.fori_loop(1, groups, drain, 0)


def per_device(
    tokens,
    norm1_gain,
    query_weight,
    key_weight,
    value_weight,
    output_weight,
    pattern,
    adjacency,
    decay_rate,
    norm2_gain,
    up_weight,
    down_weight,
):
    groups = lax.axis_size("tm")
    parts = lax.axis_size("mp")
    count, features = tokens.shape
    width = query_weight.shape[1]
    sites = adjacency.shape[0]
    steps = count // sites
    assert steps == 2
    cols = features // parts
    units = up_weight.shape[1]
    spans = [1 << k for k in range(pattern.shape[1] - 2) if 1 << k < groups]
    far = len(spans) - 1
    each = sites // groups
    slot = max(8, each)
    rows = steps * slot
    bf16, f32 = jnp.bfloat16, jnp.float32

    vmem = pl.BlockSpec(memory_space=pltpu.VMEM)
    smem = pl.BlockSpec(memory_space=pltpu.SMEM)
    hbm = pl.BlockSpec(memory_space=pl.ANY)
    others = max(1, parts - 1)
    dma = pltpu.SemaphoreType.DMA
    return pl.pallas_call(
        functools.partial(kernel, groups, parts, spans, rows, slot),
        out_shape=jax.ShapeDtypeStruct((count, cols), bf16),
        in_specs=[smem] + [hbm] * 11,
        out_specs=vmem,
        scratch_shapes=[
            pltpu.VMEM((count, features), bf16),
            pltpu.VMEM((1, features), f32),
            pltpu.VMEM((1, features), f32),
            pltpu.VMEM((1, cols), f32),
            pltpu.VMEM((sites, sites), jnp.int32),
            pltpu.VMEM((groups * rows, count), bf16),
            pltpu.VMEM((count, groups * rows), bf16),
            pltpu.VMEM((features, 3 * width), bf16),
            pltpu.VMEM((width, features), bf16),
            pltpu.VMEM((features, units), bf16),
            pltpu.VMEM((units, features), bf16),
            pltpu.VMEM((count, features), bf16),
            pltpu.VMEM((count, width), bf16),
            pltpu.VMEM((4 + far, sites, 2 * width), bf16),
            pltpu.VMEM((count, cols), bf16),
            pltpu.VMEM((parts, (2 + far) * sites, cols), bf16),
            pltpu.VMEM((max(1, far), sites, cols), bf16),
            pltpu.VMEM((width // HD, count, HD), f32),
            pltpu.VMEM((width // HD, count, HD), f32),
            pltpu.VMEM((count, width), f32),
            pltpu.VMEM((count, width), bf16),
            pltpu.VMEM((others, count, cols), bf16),
            pltpu.VMEM((others, count, cols), bf16),
            pltpu.VMEM((count, cols), bf16),
            pltpu.VMEM((groups * rows, cols), bf16),
            pltpu.VMEM((groups * rows, cols), bf16),
            pltpu.VMEM((groups * rows, cols), bf16),
            pltpu.VMEM((groups * rows, cols), bf16),
            pltpu.VMEM((parts, count, cols), bf16),
            pltpu.VMEM((count, units), bf16),
            pltpu.VMEM((others, count, cols), bf16),
            pltpu.VMEM((others, count, cols), bf16),
            dma((5,)),
            dma((6,)),
            dma((len(spans),)),
            dma((len(spans),)),
            dma((len(spans), others)),
            dma((len(spans), others)),
            dma((others,)),
            dma((others,)),
            dma((groups,)),
            dma((groups,)),
            dma((groups,)),
            dma((groups,)),
            dma((others,)),
            dma((others,)),
            dma((others,)),
            dma((others,)),
        ],
        compiler_params=pltpu.CompilerParams(
            collective_id=0, has_side_effects=True, vmem_limit_bytes=60 * 1024 * 1024
        ),
    )(
        pattern.T,
        tokens,
        norm1_gain.reshape(1, -1),
        norm2_gain.reshape(1, -1),
        decay_rate.reshape(1, -1),
        adjacency,
        query_weight,
        key_weight,
        value_weight,
        output_weight,
        up_weight,
        down_weight,
    )


def solution(mesh):
    placed = (
        P("tm", None),
        P(),
        P(None, "mp"),
        P(None, "mp"),
        P(None, "mp"),
        P("mp", None),
        P(),
        P(),
        P("mp"),
        P(),
        P(None, "mp"),
        P("mp", None),
    )
    return jax.shard_map(
        per_device, mesh=mesh, in_specs=placed, out_specs=P("tm", "mp"), check_vma=False
    )
```

```python
import functools
import math

import jax
import jax.numpy as jnp
from jax import lax
from jax.experimental import pallas as pl
from jax.experimental.pallas import tpu as pltpu
from jax.sharding import PartitionSpec as P

HD = 128
MESH = pl.DeviceIdType.MESH


def dot(a, b):
    return jnp.dot(a, b, preferred_element_type=jnp.float32)


def kernel(
    groups,
    parts,
    spans,
    rows,
    slot,
    pattern,
    tokens_in,
    gain1_in,
    gain2_in,
    decay_in,
    adjacency_in,
    wq,
    wk,
    wv,
    wo,
    wu,
    wd,
    out,
    tokens,
    gain1,
    gain2,
    decay,
    adjacency,
    spread,
    gather,
    qkv_w,
    out_w,
    up_w,
    down_w,
    normed,
    queries,
    kv,
    shared,
    far,
    sel,
    tops,
    totals,
    acc,
    attended,
    proj_send,
    proj_recv,
    first,
    mix,
    got,
    smooth,
    back,
    second,
    hidden,
    ff_send,
    ff_recv,
    in_sem,
    w_sem,
    far_s,
    far_r,
    pass_s,
    pass_r,
    proj_s,
    proj_r,
    mix_s,
    mix_r,
    back_s,
    back_r,
    sec_s,
    sec_r,
    ff_s,
    ff_r,
):
    g = lax.axis_index("tm")
    m = lax.axis_index("mp")
    sites = kv.shape[1]
    width = kv.shape[2] // 2
    heads = width // HD
    cols = out.shape[1]
    units = hidden.shape[1]

    inputs = [
        pltpu.make_async_copy(tokens_in, tokens, in_sem.at[0]),
        pltpu.make_async_copy(gain1_in, gain1, in_sem.at[1]),
        pltpu.make_async_copy(gain2_in, gain2, in_sem.at[2]),
        pltpu.make_async_copy(decay_in, decay, in_sem.at[3]),
        pltpu.make_async_copy(adjacency_in, adjacency, in_sem.at[4]),
    ]
    for load in inputs:
        load.start()
    loads = [
        pltpu.make_async_copy(wk, qkv_w.at[:, pl.ds(0, width)], w_sem.at[0]),
        pltpu.make_async_copy(wv, qkv_w.at[:, pl.ds(width, width)], w_sem.at[1]),
        pltpu.make_async_copy(wq, qkv_w.at[:, pl.ds(2 * width, width)], w_sem.at[2]),
        pltpu.make_async_copy(wo, out_w, w_sem.at[3]),
        pltpu.make_async_copy(wu, up_w, w_sem.at[4]),
        pltpu.make_async_copy(wd, down_w, w_sem.at[5]),
    ]
    for load in loads:
        load.start()

    barrier = pltpu.get_barrier_semaphore()

    def greet(step, carry):
        pl.semaphore_signal(
            barrier, inc=1, device_id=(lax.rem(g + step, groups), m), device_id_type=MESH
        )
        return carry

    lax.fori_loop(1, groups, greet, 0)
    for step in range(1, parts):
        pl.semaphore_signal(
            barrier, inc=1, device_id=(g, lax.rem(m + step, parts)), device_id_type=MESH
        )

    for load in inputs:
        load.wait()
    own = pl.ds(pl.multiple_of(m * cols, cols), cols)
    shared[...] = tokens[:, own]
    for i, span in enumerate(spans[1:]):
        target = jnp.minimum(g + span, groups - 1)
        pick = lax.rem(jnp.maximum(pattern[3 + i, 2 * target], 0), 2).astype(jnp.float32)
        sel[i] = (
            shared[:sites].astype(jnp.float32) * (1.0 - pick)
            + shared[sites:].astype(jnp.float32) * pick
        ).astype(jnp.bfloat16)

    def peer_of(step):
        return lax.rem(m + step, parts)

    def far_rows(i):
        return pl.ds(0, 2 * sites) if i == 0 else pl.ds((1 + i) * sites, sites)

    def far_copy(i):
        return pltpu.make_async_remote_copy(
            src_ref=shared if i == 0 else sel.at[i - 1],
            dst_ref=far.at[m, far_rows(i)],
            send_sem=far_s.at[i],
            recv_sem=far_r.at[i],
            device_id=(jnp.minimum(g + spans[i], groups - 1), m),
            device_id_type=MESH,
        )

    def pass_copy(i, step, part):
        return pltpu.make_async_remote_copy(
            src_ref=far.at[m, far_rows(i)],
            dst_ref=far.at[part, far_rows(i)],
            send_sem=pass_s.at[i, step - 1],
            recv_sem=pass_r.at[i, step - 1],
            device_id=(g, peer_of(step)),
            device_id_type=MESH,
        )

    pl.semaphore_wait(barrier, groups + parts - 2)
    for i in range(len(spans)):

        @pl.when(g + spans[i] < groups)
        def _(i=i):
            far_copy(i).start()

    wide = tokens[...].astype(jnp.float32)
    square = jnp.mean(wide * wide, axis=-1, keepdims=True)
    normed[...] = (wide * lax.rsqrt(square + 1e-05) * gain1[...]).astype(jnp.bfloat16)

    for j in range(2):
        loads[j].wait()
        product = dot(normed[...], qkv_w[:, pl.ds(j * width, width)]).astype(jnp.bfloat16)
        kv[0, :, pl.ds(j * width, width)] = product[:sites]
        kv[1, :, pl.ds(j * width, width)] = product[sites:]
    loads[2].wait()
    queries[...] = dot(normed[...], qkv_w[:, pl.ds(2 * width, width)]).astype(jnp.bfloat16)

    each = sites // groups
    line = lax.broadcasted_iota(jnp.int32, adjacency.shape, 0)
    other = lax.broadcasted_iota(jnp.int32, adjacency.shape, 1)
    links = jnp.where(line == other, 1, adjacency[...]).astype(jnp.float32).astype(jnp.bfloat16)
    for step in range(2):
        packed = lax.broadcasted_iota(jnp.int32, (groups * rows, sites), 0)
        site = lax.broadcasted_iota(jnp.int32, (groups * rows, sites), 1)
        inner = packed % rows
        spot = inner % slot
        here = (inner // slot == step) & (spot < each) & (packed // rows * each + spot == site)
        spread[:, pl.ds(step * sites, sites)] = dot(
            jnp.where(here, 1.0, 0.0).astype(jnp.bfloat16), links
        ).astype(jnp.bfloat16)
        site = lax.broadcasted_iota(jnp.int32, (sites, groups * rows), 0)
        packed = lax.broadcasted_iota(jnp.int32, (sites, groups * rows), 1)
        inner = packed % rows
        spot = inner % slot
        here = (inner // slot == step) & (spot < each) & (packed // rows * each + spot == site)
        gather[pl.ds(step * sites, sites), :] = jnp.where(here, 1.0, 0.0).astype(jnp.bfloat16)
    degree = jnp.maximum(
        jnp.sum(spread[...].astype(jnp.float32), axis=-1, keepdims=True), 1.0
    )

    scale = 1.0 / math.sqrt(HD)

    def attend(start, count, hide, fresh):
        for h in range(heads):
            at = pl.ds(h * HD, HD)
            keys = kv[pl.ds(start, count), :, at].reshape(count * sites, HD)
            values = kv[pl.ds(start, count), :, pl.ds(width + h * HD, HD)].reshape(
                count * sites, HD
            )
            scores = (
                lax.dot_general(
                    queries[:, at],
                    keys,
                    (((1,), (1,)), ((), ())),
                    preferred_element_type=jnp.float32,
                )
                * scale
            )
            if hide is not None:
                step = lax.broadcasted_iota(jnp.int32, scores.shape, 0) // sites
                block = lax.broadcasted_iota(jnp.int32, scores.shape, 1) // sites
                scores = jnp.where((step == hide[0]) & (block == hide[1]), -jnp.inf, scores)
            top = jnp.max(scores, axis=-1, keepdims=True)
            if fresh:
                probs = jnp.exp(scores - top)
                total = jnp.sum(probs, axis=-1, keepdims=True)
                part = dot(probs.astype(jnp.bfloat16), values)
            else:
                old = tops[h][:, :1]
                top = jnp.maximum(top, old)
                factor = jnp.exp(old - top)
                probs = jnp.exp(scores - top)
                total = totals[h][:, :1] * factor + jnp.sum(probs, axis=-1, keepdims=True)
                part = acc[:, at] * factor + dot(probs.astype(jnp.bfloat16), values)
            tops[h] = jnp.broadcast_to(top, tops.shape[1:])
            totals[h] = jnp.broadcast_to(total, totals.shape[1:])
            acc[:, at] = part

    def hand_on(i):
        @pl.when(g >= spans[i])
        def _():
            far_copy(i).wait_recv()
            for step in range(1, parts):
                pass_copy(i, step, m).start()

    def absorb(i):
        at_rows = far_rows(i)
        blocks = 2 if i == 0 else 1
        start = 2 if i == 0 else 3 + i

        @pl.when(g >= spans[i])
        def _():
            for step in range(1, parts):
                pass_copy(i, step, lax.rem(m - step + parts, parts)).wait_recv()
            square = 0.0
            for j in range(parts):
                wide = far[j, at_rows].astype(jnp.float32)
                square = square + jnp.sum(wide * wide, axis=-1, keepdims=True)
            factor = lax.rsqrt(square * (1.0 / (parts * cols)) + 1e-05)
            count = blocks * sites
            for j in range(parts):
                at = pl.ds(j * cols, cols)
                normed[pl.ds(0, count), at] = (
                    far[j, at_rows].astype(jnp.float32) * factor * gain1[:, at]
                ).astype(jnp.bfloat16)
            for j in range(2):
                at = pl.ds(j * width, width)
                product = dot(normed[pl.ds(0, count), :], qkv_w[:, at]).astype(jnp.bfloat16)
                for block in range(blocks):
                    kv[start + block, :, at] = product[block * sites : (block + 1) * sites]
            attend(start, blocks, (1, 1) if i == 0 else None, False)

    hand_on(0)
    attend(0, 2, (0, 1), True)
    for i in range(1, len(spans)):
        hand_on(i)
        absorb(i - 1)
    absorb(len(spans) - 1)

    for h in range(heads):
        at = pl.ds(h * HD, HD)
        attended[:, at] = (acc[:, at] / totals[h][:, :1]).astype(jnp.bfloat16)

    def peer_columns(step):
        return pl.ds(pl.multiple_of(peer_of(step) * cols, cols), cols)

    def proj_copy(step):
        return pltpu.make_async_remote_copy(
            src_ref=proj_send.at[step - 1],
            dst_ref=proj_recv.at[step - 1],
            send_sem=proj_s.at[step - 1],
            recv_sem=proj_r.at[step - 1],
            device_id=(g, peer_of(step)),
            device_id_type=MESH,
        )

    loads[3].wait()
    for step in range(1, parts):
        proj_send[step - 1] = dot(attended[...], out_w[:, peer_columns(step)]).astype(jnp.bfloat16)
        proj_copy(step).start()
    summed = shared[...].astype(jnp.float32) + dot(attended[...], out_w[:, own])
    for step in range(1, parts):
        proj_copy(step).wait_recv()
        summed = summed + proj_recv[step - 1].astype(jnp.float32)
    first[...] = summed.astype(jnp.bfloat16)

    mix[...] = (dot(spread[...], first[...]) / degree).astype(jnp.bfloat16)

    def share(index):
        return pl.ds(pl.multiple_of(index * rows, rows), rows)

    def mix_copy(step):
        peer = lax.rem(g + step, groups)
        return pltpu.make_async_remote_copy(
            src_ref=mix.at[share(peer)],
            dst_ref=got.at[share(g)],
            send_sem=mix_s.at[step],
            recv_sem=mix_r.at[step],
            device_id=(peer, m),
            device_id_type=MESH,
        )

    def mix_start(step, carry):
        mix_copy(step).start()
        return carry

    lax.fori_loop(1, groups, mix_start, 0)
    got[share(g)] = mix[share(g)]

    def back_copy(step):
        peer = lax.rem(g + step, groups)
        return pltpu.make_async_remote_copy(
            src_ref=smooth.at[share(peer)],
            dst_ref=back.at[share(g)],
            send_sem=back_s.at[step],
            recv_sem=back_r.at[step],
            device_id=(peer, m),
            device_id_type=MESH,
        )

    retain = jnp.exp(-decay[...])
    inject = jnp.sqrt(1.0 - retain * retain)

    def advance(index, state):
        @pl.when(index != g)
        def _():
            step = lax.rem(g - index + groups, groups)
            pltpu.make_async_remote_copy(
                src_ref=mix.at[share(index)],
                dst_ref=got.at[share(index)],
                send_sem=mix_s.at[step],
                recv_sem=mix_r.at[step],
                device_id=(index, m),
                device_id_type=MESH,
            ).wait_recv()

        frames = got[share(index)].astype(jnp.float32)
        early = retain * state + inject * frames[:slot]
        late = retain * early + inject * frames[slot:]
        smooth[share(index)] = jnp.concatenate([early, late], axis=0).astype(jnp.bfloat16)

        @pl.when(index != g)
        def _():
            back_copy(lax.rem(index - g + groups, groups)).start()

        return late

    lax.fori_loop(0, groups, advance, jnp.zeros((slot, cols), jnp.float32))
    back[share(g)] = smooth[share(g)]

    def back_wait(step, carry):
        source = lax.rem(g - step + groups, groups)
        pltpu.make_async_remote_copy(
            src_ref=smooth.at[share(source)],
            dst_ref=back.at[share(source)],
            send_sem=back_s.at[step],
            recv_sem=back_r.at[step],
            device_id=(source, m),
            device_id_type=MESH,
        ).wait_recv()
        return carry

    lax.fori_loop(1, groups, back_wait, 0)

    second[m] = (first[...].astype(jnp.float32) + dot(gather[...], back[...])).astype(jnp.bfloat16)

    def second_copy(step, slot_of):
        return pltpu.make_async_remote_copy(
            src_ref=second.at[m],
            dst_ref=second.at[slot_of],
            send_sem=sec_s.at[step - 1],
            recv_sem=sec_r.at[step - 1],
            device_id=(g, peer_of(step)),
            device_id_type=MESH,
        )

    for step in range(1, parts):
        second_copy(step, m).start()
    for step in range(1, parts):
        second_copy(step, lax.rem(m - step + parts, parts)).wait_recv()

    square = 0.0
    for j in range(parts):
        wide = second[j].astype(jnp.float32)
        square = square + jnp.sum(wide * wide, axis=-1, keepdims=True)
    factor = lax.rsqrt(square * (1.0 / (parts * cols)) + 1e-05)
    for j in range(parts):
        at = pl.ds(j * cols, cols)
        normed[:, at] = (second[j].astype(jnp.float32) * factor * gain2[:, at]).astype(jnp.bfloat16)

    tile = min(512, units)
    loads[4].wait()

    def expand(index, carry):
        at = pl.ds(pl.multiple_of(index * tile, tile), tile)
        hidden[:, at] = jax.nn.gelu(dot(normed[...], up_w[:, at]), approximate=True).astype(
            jnp.bfloat16
        )
        return carry

    lax.fori_loop(0, units // tile, expand, 0)

    def ff_copy(step):
        return pltpu.make_async_remote_copy(
            src_ref=ff_send.at[step - 1],
            dst_ref=ff_recv.at[step - 1],
            send_sem=ff_s.at[step - 1],
            recv_sem=ff_r.at[step - 1],
            device_id=(g, peer_of(step)),
            device_id_type=MESH,
        )

    loads[5].wait()
    for step in range(1, parts):
        ff_send[step - 1] = dot(hidden[...], down_w[:, peer_columns(step)]).astype(jnp.bfloat16)
        ff_copy(step).start()
    summed = second[m].astype(jnp.float32) + dot(hidden[...], down_w[:, own])
    for step in range(1, parts):
        ff_copy(step).wait_recv()
        summed = summed + ff_recv[step - 1].astype(jnp.float32)
    out[...] = summed.astype(jnp.bfloat16)

    for i, span in enumerate(spans):

        @pl.when(g + span < groups)
        def _(i=i):
            far_copy(i).wait_send()

        @pl.when(g >= span)
        def _(i=i):
            for step in range(1, parts):
                pass_copy(i, step, m).wait_send()

    for step in range(1, parts):
        proj_copy(step).wait_send()
        second_copy(step, m).wait_send()
        ff_copy(step).wait_send()

    def drain(step, carry):
        mix_copy(step).wait_send()
        back_copy(step).wait_send()
        return carry

    lax.fori_loop(1, groups, drain, 0)


def per_device(
    tokens,
    norm1_gain,
    query_weight,
    key_weight,
    value_weight,
    output_weight,
    pattern,
    adjacency,
    decay_rate,
    norm2_gain,
    up_weight,
    down_weight,
):
    groups = lax.axis_size("tm")
    parts = lax.axis_size("mp")
    count, features = tokens.shape
    width = query_weight.shape[1]
    sites = adjacency.shape[0]
    steps = count // sites
    assert steps == 2
    cols = features // parts
    units = up_weight.shape[1]
    spans = [1 << k for k in range(pattern.shape[1] - 2) if 1 << k < groups]
    far = len(spans) - 1
    each = sites // groups
    slot = max(8, each)
    rows = steps * slot
    bf16, f32 = jnp.bfloat16, jnp.float32

    vmem = pl.BlockSpec(memory_space=pltpu.VMEM)
    smem = pl.BlockSpec(memory_space=pltpu.SMEM)
    hbm = pl.BlockSpec(memory_space=pl.ANY)
    others = max(1, parts - 1)
    dma = pltpu.SemaphoreType.DMA
    return pl.pallas_call(
        functools.partial(kernel, groups, parts, spans, rows, slot),
        out_shape=jax.ShapeDtypeStruct((count, cols), bf16),
        in_specs=[smem] + [hbm] * 11,
        out_specs=vmem,
        scratch_shapes=[
            pltpu.VMEM((count, features), bf16),
            pltpu.VMEM((1, features), f32),
            pltpu.VMEM((1, features), f32),
            pltpu.VMEM((1, cols), f32),
            pltpu.VMEM((sites, sites), jnp.int32),
            pltpu.VMEM((groups * rows, count), bf16),
            pltpu.VMEM((count, groups * rows), bf16),
            pltpu.VMEM((features, 3 * width), bf16),
            pltpu.VMEM((width, features), bf16),
            pltpu.VMEM((features, units), bf16),
            pltpu.VMEM((units, features), bf16),
            pltpu.VMEM((count, features), bf16),
            pltpu.VMEM((count, width), bf16),
            pltpu.VMEM((4 + far, sites, 2 * width), bf16),
            pltpu.VMEM((count, cols), bf16),
            pltpu.VMEM((parts, (2 + far) * sites, cols), bf16),
            pltpu.VMEM((max(1, far), sites, cols), bf16),
            pltpu.VMEM((width // HD, count, HD), f32),
            pltpu.VMEM((width // HD, count, HD), f32),
            pltpu.VMEM((count, width), f32),
            pltpu.VMEM((count, width), bf16),
            pltpu.VMEM((others, count, cols), bf16),
            pltpu.VMEM((others, count, cols), bf16),
            pltpu.VMEM((count, cols), bf16),
            pltpu.VMEM((groups * rows, cols), bf16),
            pltpu.VMEM((groups * rows, cols), bf16),
            pltpu.VMEM((groups * rows, cols), bf16),
            pltpu.VMEM((groups * rows, cols), bf16),
            pltpu.VMEM((parts, count, cols), bf16),
            pltpu.VMEM((count, units), bf16),
            pltpu.VMEM((others, count, cols), bf16),
            pltpu.VMEM((others, count, cols), bf16),
            dma((5,)),
            dma((6,)),
            dma((len(spans),)),
            dma((len(spans),)),
            dma((len(spans), others)),
            dma((len(spans), others)),
            dma((others,)),
            dma((others,)),
            dma((groups,)),
            dma((groups,)),
            dma((groups,)),
            dma((groups,)),
            dma((others,)),
            dma((others,)),
            dma((others,)),
            dma((others,)),
        ],
        compiler_params=pltpu.CompilerParams(
            collective_id=0, has_side_effects=True, vmem_limit_bytes=60 * 1024 * 1024
        ),
    )(
        pattern.T,
        tokens,
        norm1_gain.reshape(1, -1),
        norm2_gain.reshape(1, -1),
        decay_rate.reshape(1, -1),
        adjacency,
        query_weight,
        key_weight,
        value_weight,
        output_weight,
        up_weight,
        down_weight,
    )


def solution(mesh):
    placed = (
        P("tm", None),
        P(),
        P(None, "mp"),
        P(None, "mp"),
        P(None, "mp"),
        P("mp", None),
        P(),
        P(),
        P("mp"),
        P(),
        P(None, "mp"),
        P("mp", None),
    )
    return jax.shard_map(
        per_device, mesh=mesh, in_specs=placed, out_specs=P("tm", "mp"), check_vma=False
    )
```
